256 devices in a mesh: blk: 32 (over z, x), head: 2 (over core), rep: 4 (over y).
Axes of the slice: x: 4, y: 4, z: 8, core: 2. Of those that a mesh axis runs over, the one named last changes fastest.
Arguments:
- queries: bfloat16 [4096, 4096], P(('rep', 'blk'), 'head'), parts along dimension 0, may hold values from -400 to 400
- cache_keys: bfloat16 [131072, 256], P(('rep', 'blk'), 'head'), parts along dimension 0, may hold values from -6 to 6
- cache_values: bfloat16 [131072, 256], P(('rep', 'blk'), 'head'), parts along dimension 0, may hold values from -6 to 6
- slot_request: int32 [131072], P(('rep', 'blk')), parts along dimension 0, may hold values from 0 to 1, as said below
- slot_position: int32 [131072], P(('rep', 'blk')), parts along dimension 0, may hold values from 0 to 16383
- lengths: int32 [8], P('rep'), parts along dimension 0, may hold values from 8192 to 16384, as said below
- query_request: int32 [4096], P(('rep', 'blk')), parts along dimension 0, may hold values from 0 to 1
- query_offset: int32 [4096], P(('rep', 'blk')), parts along dimension 0, may hold values from 0 to 511
Outputs:
- attended: bfloat16 [4096, 4096], P(('rep', 'blk'), 'head'), parts along dimension 0
The draws below stay inside these ranges and needn't reach their ends.
There are 4 independent parts, one for each index of `rep`. The reference program is written for one: setup_inputs(seed, part) draws one part's arguments, and reference() takes and returns one part's arrays. A program takes and returns all parts, laid end to end along the dimension named above; each array names one. Nothing has to cross between parts.
Inputs may be any that keep to these rules, and one draw needn't show every extreme that they name: `slot_request`: every pair of a request below 2 and a position below 16384 stands in exactly one slot. `lengths`: some request has length 16384.
All inputs are finite; a program needn't handle non-finite values.
Results may differ from the reference program's by a relative error of at most 0.0065.
Values may be sent and summed in bfloat16 or wider, within the bound.
A program may use at most 64 MiB of HBM per device.

```python
import jax
import jax.numpy as jnp
from jax import lax

HD = 128
QH_DEV = 16
Q_DEV = 32
REQS = 2
KVH = 2
HQ = 32
SLOTS = 32768
CAP = 16384
Q_TOT = 1024
NEW = 512


def slot_layout(key):
    order = jax.random.permutation(jax.random.fold_in(key, 11), SLOTS)
    ranks = jnp.arange(SLOTS, dtype=jnp.int32)
    request = jnp.zeros((SLOTS,), jnp.int32).at[order].set(ranks // CAP)
    position = jnp.zeros((SLOTS,), jnp.int32).at[order].set(ranks % CAP)
    return (request, position)


def draw_slot_request(key, part):
    layout = slot_layout(key)
    return layout[0]


def draw_slot_position(key, part):
    layout = slot_layout(key)
    return layout[1]


def draw_lengths(key, part):
    key = jax.random.fold_in(key, 3)
    first, second = jax.random.split(key, 2)
    drawn = jax.random.randint(first, (REQS,), CAP // 2, CAP)
    longest = jax.random.randint(second, (), 0, REQS)
    return drawn.at[longest].set(CAP).astype(jnp.int32)


def draw_queries(key, part):
    key = jax.random.fold_in(key, 5)
    base = jnp.clip(jax.random.normal(key, (Q_TOT, HQ * HD), jnp.float32) * 2.5, -16.0, 16.0)
    return base.astype(jnp.bfloat16)


def place_ends(values, key, least, high):
    shape = values.shape
    spot = [jax.random.randint(jax.random.fold_in(key, axis), (), 0, shape[axis]) for axis in range(len(shape))]
    values = values.at[tuple(spot)].set(least)
    longest = shape.index(max(shape))
    spot[longest] = (spot[longest] + 1) % shape[longest]
    return values.at[tuple(spot)].set(high)


def steps_of(key, shape, shards, least, high):
    def one(dim, blocks):
        heights = jax.random.uniform(jax.random.fold_in(jax.random.fold_in(key, 6), dim), (blocks,), jnp.float32, least / len(shards), high / len(shards))
        return jnp.repeat(jnp.exp(heights), shape[dim] // blocks).reshape((-1,) + (1,) * (len(shape) - dim - 1))

    factor_of = one(*shards[0])
    for cut in shards[1:]:
        factor_of = factor_of * one(*cut)
    return factor_of


def bell_draw(stream_key, extent, width, limit, pieces=(), kind=jnp.bfloat16):
    level = steps_of(stream_key, extent, pieces, -0.22, 0.18) if pieces else 1.0
    values = jax.random.normal(stream_key, extent, jnp.float32) * width * level
    return jnp.minimum(jnp.maximum(values, -limit), limit).astype(kind)


def setup_inputs(seed: int = 0, part: int = 0) -> dict:
    key_of = jax.random.split(jax.random.key(seed), 9)
    part_keys = jax.random.split(jax.random.fold_in(key_of[8], part), 9)
    queries = draw_queries(jax.random.fold_in(jax.random.fold_in(key_of[8], part), 71), part)
    cache_keys = bell_draw(part_keys[1], (SLOTS, KVH * HD), 1.0, 6.0, ((0, 32), (1, 2)))
    cache_values = bell_draw(part_keys[2], (SLOTS, KVH * HD), 1.0, 6.0, ((0, 32), (1, 2)))
    slot_request = draw_slot_request(jax.random.fold_in(jax.random.fold_in(key_of[8], part), 71), part)
    slot_position = draw_slot_position(jax.random.fold_in(jax.random.fold_in(key_of[8], part), 71), part)
    lengths = draw_lengths(jax.random.fold_in(jax.random.fold_in(key_of[8], part), 71), part)
    query_request = place_ends(jax.random.randint(part_keys[6], (Q_TOT,), 0, REQS), jax.random.fold_in(part_keys[6], 1), 0, REQS - 1).astype(jnp.int32)
    query_offset = place_ends(jax.random.randint(part_keys[7], (Q_TOT,), 0, NEW), jax.random.fold_in(part_keys[7], 1), 0, NEW - 1).astype(jnp.int32)
    return {"queries": queries, "cache_keys": cache_keys, "cache_values": cache_values, "slot_request": slot_request, "slot_position": slot_position, "lengths": lengths, "query_request": query_request, "query_offset": query_offset}


masked_score = -1e30


def reference(queries, cache_keys, cache_values, slot_request, slot_position, lengths, query_request, query_offset):
    match = query_request[:, None] == jnp.arange(REQS, dtype=jnp.int32)[None, :]
    own_length = jnp.sum(jnp.where(match, lengths[None, :], 0), axis=1).astype(jnp.int32)
    query_position = own_length - 1 - query_offset
    head_count = cache_keys.shape[1] // HD

    def one_head(head_index):
        key_rows = lax.dynamic_slice_in_dim(cache_keys, head_index * HD, HD, 1).astype(jnp.float32)
        value_rows = lax.dynamic_slice_in_dim(cache_values, head_index * HD, HD, 1).astype(jnp.float32)
        query_cols = lax.dynamic_slice_in_dim(queries, head_index * QH_DEV * HD, QH_DEV * HD, 1)

        def one_block(block_index):
            begin_row = block_index * Q_DEV
            query_block = lax.dynamic_slice_in_dim(query_cols, begin_row, Q_DEV, 0)
            query_block = query_block.reshape(Q_DEV, QH_DEV, HD).astype(jnp.float32)
            block_request = lax.dynamic_slice_in_dim(query_request, begin_row, Q_DEV, 0)
            block_position = lax.dynamic_slice_in_dim(query_position, begin_row, Q_DEV, 0)
            scores = jnp.einsum("qgd,kd->qgk", query_block, key_rows) * (HD ** -0.5)
            allowed = (block_request[:, None] == slot_request[None, :]) & (slot_position[None, :] <= block_position[:, None])
            scores = jnp.where(allowed[:, None, :], scores, masked_score)
            peak_score = jnp.max(scores, axis=2)
            raw_weight = jnp.where(allowed[:, None, :], jnp.exp(scores - peak_score[:, :, None]), 0.0)
            weight_sum = jnp.sum(raw_weight, axis=2)
            weights = raw_weight.astype(jnp.bfloat16).astype(jnp.float32)
            weighted = jnp.einsum("qgk,kd->qgd", weights, value_rows)
            return (weighted / weight_sum[:, :, None]).reshape(Q_DEV, QH_DEV * HD)

        block_outs = lax.map(one_block, jnp.arange(Q_TOT // Q_DEV, dtype=jnp.int32))
        return block_outs.reshape(Q_TOT, QH_DEV * HD)

    head_outs = lax.map(one_head, jnp.arange(head_count, dtype=jnp.int32))
    return jnp.transpose(head_outs, (1, 0, 2)).reshape(Q_TOT, head_count * QH_DEV * HD).astype(jnp.bfloat16)
```

```python
import functools

import jax
import jax.numpy as jnp
from jax import lax
from jax.experimental import pallas as pl
from jax.experimental.pallas import tpu as pltpu
from jax.sharding import PartitionSpec as P

HD = 128
QH_DEV = 16
TOK = 32
ROWS = TOK * QH_DEV
SLOT = 1024
HALF = SLOT // 2
QW = QH_DEV * HD
NZ = 8
NX = 4
SCALE = 1.4426950408889634 * HD ** -0.5
MASKED = -1e30
FLOOR = -1e29
REQ_STEP = 65536.0
SOFT_ROWS = 128
MESH = pl.DeviceIdType.MESH
F32 = jnp.float32
BF16 = jnp.bfloat16

PAIRS = (
    (0, 0), (1, 0), (7, 0), (0, 1), (1, 1), (7, 1), (2, 0), (6, 0),
    (2, 1), (6, 1), (3, 0), (5, 0), (3, 1), (5, 1), (4, 0), (4, 1),
    (4, 2), (4, 3), (3, 2), (3, 3), (5, 2), (5, 3), (2, 2), (2, 3),
    (6, 2), (6, 3), (1, 2), (1, 3), (7, 2), (7, 3), (0, 2), (0, 3),
)
N = len(PAIRS)


def first_use(kind, value):
    return min(i for i, pair in enumerate(PAIRS) if pair[kind] == value)


def last_use(query):
    return max(i for i, pair in enumerate(PAIRS) if pair[0] == query)


def pick(index, column):
    value = jnp.int32(PAIRS[N - 1][column])
    for i in range(N - 2, -1, -1):
        value = jnp.where(index <= i, jnp.int32(PAIRS[i][column]), value)
    return value


def kernel(
    len_ref, qreq_ref, qoff_ref, sreq_ref, spos_ref, q_hbm, k_hbm, v_hbm,
    out_ref,
    qs, ks, vs, code, s0, s1, p0, p1, a0, a1, acc, peak,
    sent, sent_stat, got, got_stat,
    local_sem, kv_send, kv_recv, q_send, q_recv, part_send, part_recv,
):
    me = lax.axis_index("blk")
    z = me // NX
    x = lax.rem(me, NX)
    right = z * NX + lax.rem(x + 1, NX)
    left = z * NX + lax.rem(x + NX - 1, NX)
    up = lax.rem(z + 1, NZ) * NX + x
    down = lax.rem(z + NZ - 1, NZ) * NX + x

    barrier = pltpu.get_barrier_semaphore()
    for other in (up, down, right, left):
        pl.semaphore_signal(barrier, inc=1, device_id={"blk": other}, device_id_type=MESH)

    own = [
        pltpu.make_async_copy(q_hbm, qs.at[0, :, pl.ds(0, QW)], local_sem.at[0]),
        pltpu.make_async_copy(k_hbm, ks.at[0], local_sem.at[1]),
        pltpu.make_async_copy(v_hbm, vs.at[0, :, pl.ds(0, HD)], local_sem.at[2]),
    ]
    for copy in own:
        copy.start()

    request = qreq_ref[...]
    length = jnp.where(request == 0, len_ref[0], len_ref[1])
    position = length - 1 - qoff_ref[...]
    eye = lax.broadcasted_iota(jnp.int32, (TOK, TOK), 0) == lax.broadcasted_iota(jnp.int32, (TOK, TOK), 1)

    def column(row):
        return jnp.sum(jnp.where(eye, jnp.broadcast_to(row, (TOK, TOK)), 0), axis=1, keepdims=True)

    lane = lax.broadcasted_iota(jnp.int32, (TOK, HD), 1)
    position = column(position)
    meta = jnp.where(
        lane == 0, column(request),
        jnp.where(lane == 1, position // 128, jnp.where(lane == 2, position % 128, 0)),
    )
    qs[0, :, QW:] = meta.astype(F32).astype(BF16)
    code[0] = sreq_ref[...].astype(F32) * REQ_STEP + spos_ref[...].astype(F32)
    vs[:, :, HD:] = jnp.ones((NX, SLOT, HD), BF16)
    acc[...] = jnp.zeros_like(acc)
    peak[...] = jnp.full(peak.shape, FLOOR, F32)
    p1[...] = jnp.zeros_like(p1)
    a1[...] = jnp.ones_like(a1)
    for copy in own:
        copy.wait()
    pl.semaphore_wait(barrier, 4)

    def remote(src, dst, send_sem, recv_sem, other):
        return pltpu.make_async_remote_copy(
            src_ref=src, dst_ref=dst, send_sem=send_sem, recv_sem=recv_sem,
            device_id={"blk": other}, device_id_type=MESH,
        )

    def kv_copies(chunk, src_slot, src_at, dst_slot, dst_at, other):
        src = pl.ds(src_at, HALF)
        dst = pl.ds(dst_at, HALF)
        return [
            remote(ks.at[src_slot, src], ks.at[dst_slot, dst],
                   kv_send.at[chunk, 0], kv_recv.at[chunk, 0], other),
            remote(vs.at[src_slot, src, pl.ds(0, HD)], vs.at[dst_slot, dst, pl.ds(0, HD)],
                   kv_send.at[chunk, 1], kv_recv.at[chunk, 1], other),
            remote(code.at[src_slot, :, src], code.at[dst_slot, :, dst],
                   kv_send.at[chunk, 2], kv_recv.at[chunk, 2], other),
        ]

    kv = [
        kv_copies(0, 0, HALF, 1, 0, right),
        kv_copies(1, 0, 0, 1, HALF, left),
        kv_copies(2, 0, 0, 2, 0, right),
        kv_copies(3, 0, HALF, 2, HALF, left),
        kv_copies(4, 1, 0, 3, HALF, right),
        kv_copies(5, 1, HALF, 3, 0, left),
    ]
    qc = {
        7: remote(qs.at[0], qs.at[7], q_send.at[7], q_recv.at[7], up),
        6: remote(qs.at[7], qs.at[6], q_send.at[6], q_recv.at[6], up),
        5: remote(qs.at[6], qs.at[5], q_send.at[5], q_recv.at[5], up),
        4: remote(qs.at[5, pl.ds(0, TOK // 2)], qs.at[4, pl.ds(0, TOK // 2)],
                  q_send.at[4], q_recv.at[4], up),
        1: remote(qs.at[0], qs.at[1], q_send.at[1], q_recv.at[1], down),
        2: remote(qs.at[1], qs.at[2], q_send.at[2], q_recv.at[2], down),
        3: remote(qs.at[2], qs.at[3], q_send.at[3], q_recv.at[3], down),
        0: remote(qs.at[3, pl.ds(TOK // 2, TOK // 2)], qs.at[4, pl.ds(TOK // 2, TOK // 2)],
                  q_send.at[0], q_recv.at[0], down),
    }
    def part_copies(src_slot, dst_slot, begin, count, other):
        rows = pl.ds(begin, count)
        stats = pl.ds(begin // HD, count // HD)
        return [
            remote(sent.at[src_slot, rows], got.at[dst_slot, rows],
                   part_send.at[dst_slot, 0], part_recv.at[dst_slot, 0], other),
            remote(sent_stat.at[src_slot, stats], got_stat.at[dst_slot, stats],
                   part_send.at[dst_slot, 1], part_recv.at[dst_slot, 1], other),
        ]

    part = {
        3: part_copies(4, 3, 0, ROWS // 2, up),
        2: part_copies(3, 2, 0, ROWS, up),
        1: part_copies(2, 1, 0, ROWS, up),
        0: part_copies(1, 0, 0, ROWS, up),
        5: part_copies(4, 5, ROWS // 2, ROWS // 2, down),
        6: part_copies(5, 6, 0, ROWS, down),
        7: part_copies(6, 7, 0, ROWS, down),
        4: part_copies(7, 4, 0, ROWS, down),
    }

    def start(copies):
        for copy in copies:
            copy.start()

    start([qc[7], qc[1]])
    for chunk in range(4):
        start(kv[chunk])

    eye_hd = lax.broadcasted_iota(jnp.int32, (HD, HD), 0) == lax.broadcasted_iota(jnp.int32, (HD, HD), 1)

    def to_row(block):
        return jnp.sum(jnp.where(eye_hd, block, 0.0), axis=0, keepdims=True)

    def to_column(row):
        return jnp.sum(jnp.where(eye_hd, jnp.broadcast_to(row, (HD, HD)), 0.0), axis=1, keepdims=True)

    def state(query, g):
        rows = pl.ds(g * HD, HD)
        return peak[query, rows, :], acc[query, rows, 0:HD], acc[query, rows, HD:]

    def merge(mine, slot, g):
        rows = pl.ds(g * HD, HD)
        m, w, l = mine
        m_in = to_column(got_stat[slot, g, 0:1, :])
        l_in = to_column(got_stat[slot, g, 1:2, :])
        m_new = jnp.maximum(m, m_in)
        keep = jnp.exp2(m - m_new)
        take = jnp.exp2(m_in - m_new)
        return m_new, w * keep + got[slot, rows, :].astype(F32) * take, l * keep + l_in * take

    def finish(query):
        if query == 3:
            merged = (0, 1)
        elif query == 5:
            merged = (2, 3)
        elif query == 4:
            merged = ()
        else:
            merged = (0, 1, 2, 3)
        if merged:
            for copy in part[query]:
                copy.wait_recv()
        for g in range(4):
            now = state(query, g)
            if g in merged:
                now = merge(now, query, g)
            m, w, l = now
            sent[query, pl.ds(g * HD, HD), :] = w.astype(BF16)
            sent_stat[query, g, 0:1, :] = to_row(m)
            sent_stat[query, g, 1:2, :] = to_row(l)
        if query == 4:
            start(part[3])
            start(part[5])
        elif query < 4:
            start(part[query - 1])
        else:
            start(part[(query + 1) if query < 7 else 4])

    actions = {}

    def at(stage, action):
        actions.setdefault(stage, []).append(action)

    def take_query(low, high, forward):
        def action():
            for copy in low:
                copy.wait_recv()
            for copy in high:
                copy.wait_recv()
            start(forward)
        return action

    def take_keys(chunks):
        def action():
            for chunk in chunks:
                for copy in kv[chunk]:
                    copy.wait_recv()
        return action

    def forward_keys():
        start(kv[4])
        start(kv[5])

    at(first_use(0, 1) - 1, take_query([qc[1]], [qc[7]], [qc[2], qc[6]]))
    at(first_use(0, 2) - 1, take_query([qc[2]], [qc[6]], [qc[3], qc[5]]))
    at(first_use(0, 3) - 1, take_query([qc[3]], [qc[5]], [qc[0], qc[4]]))
    at(first_use(0, 4) - 1, take_query([qc[0]], [qc[4]], []))
    at(first_use(1, 1) - 1, take_keys((0, 1)))
    at(first_use(1, 1) - 1 + FORWARD_AFTER, forward_keys)
    at(first_use(1, 2) - 1, take_keys((2, 3)))
    at(first_use(1, 3) - 1, take_keys((4, 5)))
    for query in (4, 3, 5, 2, 6, 1, 7):
        at(last_use(query) + 2, functools.partial(finish, query))

    def do(stage_index, parity):
        for stage in sorted(actions):
            if stage % 2 == parity and stage < N:
                @pl.when(stage_index == stage)
                def _():
                    for action in actions[stage]:
                        action()

    def scores(query, key, into):
        q = jnp.concatenate([qs[query, :, pl.ds(h * HD, HD)] for h in range(QH_DEV)], axis=0)
        into[...] = lax.dot_general(q, ks[key], (((1,), (1,)), ((), ())), preferred_element_type=F32)

    def softmax(query, key, scored, weights, shrink):
        meta = qs[query, :, QW:].astype(F32)
        low = meta[:, 0:1] * REQ_STEP
        high = low + (meta[:, 1:2] * 128.0 + meta[:, 2:3])
        where = code[key]
        bias = jnp.where((where >= low) & (where <= high), 0.0, MASKED)
        for r in range(ROWS // SOFT_ROWS):
            rows = pl.ds(r * SOFT_ROWS, SOFT_ROWS)
            heads = SOFT_ROWS // TOK
            s = (scored[rows, :].reshape(heads, TOK, SLOT) * SCALE + bias[None]).reshape(SOFT_ROWS, SLOT)
            m_old = peak[query, rows, :]
            m_new = jnp.maximum(m_old, jnp.max(s, axis=1, keepdims=True))
            shrink[rows, :] = jnp.exp2(m_old - m_new)
            weights[rows, :] = jnp.exp2(s - m_new[:, 0:1]).astype(BF16)
            peak[query, rows, :] = m_new

    def values(query, key, weights, shrink):
        o = jnp.dot(weights[...], vs[key], preferred_element_type=F32)
        keep = shrink[...]
        acc[query, :, 0:HD] = acc[query, :, 0:HD] * keep + o[:, 0:HD]
        acc[query, :, HD:] = acc[query, :, HD:] * keep + o[:, HD:]

    scores(0, 0, s0)

    def body(j, carry):
        before, now = carry
        i = 2 * j
        do(i, 0)
        after = (pick(i + 1, 0), pick(i + 1, 1))
        scores(*after, s1)
        softmax(*now, s0, p0, a0)
        values(*before, p1, a1)
        do(i + 1, 1)
        last = (pick(i + 2, 0), pick(i + 2, 1))
        scores(*last, s0)
        softmax(*after, s1, p1, a1)
        values(*now, p0, a0)
        return after, last

    zero = jnp.int32(0)
    first = (zero, zero)
    lax.fori_loop(0, N // 2, body, (first, first))
    values(*PAIRS[N - 1], p1, a1)
    for stage in sorted(actions):
        if stage >= N:
            for action in actions[stage]:
                action()

    for slot in (0, 4):
        for copy in part[slot]:
            copy.wait_recv()
    for g in range(4):
        now = merge(merge(state(0, g), 0, g), 4, g)
        o = (now[1] / now[2]).astype(BF16)
        for h in range(4):
            out_ref[:, pl.ds((g * 4 + h) * HD, HD)] = o[h * TOK:(h + 1) * TOK, :]

    for copies in kv:
        for copy in copies:
            copy.wait_send()
    for copy in qc.values():
        copy.wait_send()
    for copies in part.values():
        for copy in copies:
            copy.wait_send()


FORWARD_AFTER = 4


def shards(
    queries,
    cache_keys,
    cache_values,
    slot_request,
    slot_position,
    lengths,
    query_request,
    query_offset,
):
    vmem = pl.BlockSpec(memory_space=pltpu.VMEM)
    hbm = pl.BlockSpec(memory_space=pl.ANY)
    dma = pltpu.SemaphoreType.DMA
    return pl.pallas_call(
        kernel,
        out_shape=jax.ShapeDtypeStruct((TOK, QW), BF16),
        in_specs=[pl.BlockSpec(memory_space=pltpu.SMEM), vmem, vmem, vmem, vmem, hbm, hbm, hbm],
        out_specs=vmem,
        scratch_shapes=[
            pltpu.VMEM((NZ, TOK, QW + HD), BF16),
            pltpu.VMEM((NX, SLOT, HD), BF16),
            pltpu.VMEM((NX, SLOT, 2 * HD), BF16),
            pltpu.VMEM((NX, 1, SLOT), F32),
            pltpu.VMEM((ROWS, SLOT), F32),
            pltpu.VMEM((ROWS, SLOT), F32),
            pltpu.VMEM((ROWS, SLOT), BF16),
            pltpu.VMEM((ROWS, SLOT), BF16),
            pltpu.VMEM((ROWS, HD), F32),
            pltpu.VMEM((ROWS, HD), F32),
            pltpu.VMEM((NZ, ROWS, 2 * HD), F32),
            pltpu.VMEM((NZ, ROWS, HD), F32),
            pltpu.VMEM((NZ, ROWS, HD), BF16),
            pltpu.VMEM((NZ, 4, 8, HD), F32),
            pltpu.VMEM((NZ, ROWS, HD), BF16),
            pltpu.VMEM((NZ, 4, 8, HD), F32),
            dma((3,)),
            dma((6, 3)),
            dma((6, 3)),
            dma((NZ,)),
            dma((NZ,)),
            dma((NZ, 2)),
            dma((NZ, 2)),
        ],
        compiler_params=pltpu.CompilerParams(
            collective_id=0, has_side_effects=True, vmem_limit_bytes=48 * 2 ** 20
        ),
        cost_estimate=pl.CostEstimate(
            flops=4 * ROWS * SLOT * HD * N, bytes_accessed=2 ** 20, transcendentals=ROWS * SLOT * N
        ),
        name="ring_attention",
    )(
        lengths,
        query_request.reshape(1, TOK),
        query_offset.reshape(1, TOK),
        slot_request.reshape(1, SLOT),
        slot_position.reshape(1, SLOT),
        queries,
        cache_keys,
        cache_values,
    )


def solution(mesh):
    return jax.shard_map(
        shards,
        mesh=mesh,
        in_specs=(
            P(("rep", "blk"), "head"),
            P(("rep", "blk"), "head"),
            P(("rep", "blk"), "head"),
            P(("rep", "blk")),
            P(("rep", "blk")),
            P("rep"),
            P(("rep", "blk")),
            P(("rep", "blk")),
        ),
        out_specs=P(("rep", "blk"), "head"),
        check_vma=False,
    )
```

```python
import functools

import jax
import jax.numpy as jnp
from jax import lax
from jax.experimental import pallas as pl
from jax.experimental.pallas import tpu as pltpu
from jax.sharding import PartitionSpec as P

HD = 128
QH_DEV = 16
TOK = 32
ROWS = TOK * QH_DEV
SLOT = 1024
HALF = SLOT // 2
QW = QH_DEV * HD
NZ = 8
NX = 4
SCALE = 1.4426950408889634 * HD ** -0.5
MASKED = -1e30
FLOOR = -1e29
REQ_STEP = 65536.0
SOFT_ROWS = 128
MESH = pl.DeviceIdType.MESH
F32 = jnp.float32
BF16 = jnp.bfloat16

PAIRS = (
    (0, 0), (1, 0), (7, 0), (0, 1), (1, 1), (7, 1), (4, 0), (4, 1),
    (4, 2), (1, 2), (7, 2), (3, 0), (5, 0), (3, 1), (5, 1), (3, 2),
    (5, 2), (2, 0), (3, 3), (5, 3), (4, 3), (1, 3), (7, 3), (2, 1),
    (2, 2), (2, 3), (6, 0), (6, 1), (6, 2), (6, 3), (0, 2), (0, 3),
)
N = len(PAIRS)


def first_use(kind, value):
    return min(i for i, pair in enumerate(PAIRS) if pair[kind] == value)


def last_use(query):
    return max(i for i, pair in enumerate(PAIRS) if pair[0] == query)


def kernel(
    len_hbm, qreq_hbm, qoff_hbm, sreq_hbm, spos_hbm, q_hbm, k_hbm, v_hbm,
    out_ref,
    len_ref, qreq_ref, qoff_ref, sreq_ref, spos_ref,
    qs, ks, vs, code, b0, b1, s0, s1, p0, p1, a0, a1, acc, peak,
    sent, sent_stat, got, got_stat,
    local_sem, kv_send, kv_recv, q_send, q_recv, part_send, part_recv,
):
    me = lax.axis_index("blk")
    z = me // NX
    x = lax.rem(me, NX)

    def along_z(step):
        return lax.rem(z + step + NZ, NZ) * NX + x

    right = z * NX + lax.rem(x + 1, NX)
    left = z * NX + lax.rem(x + NX - 1, NX)
    up, up2, far, down2, down = (along_z(step) for step in (1, 2, 4, -2, -1))

    barrier = pltpu.get_barrier_semaphore()
    for other in (up, down, right, left, up2, down2, far):
        pl.semaphore_signal(barrier, inc=1, device_id={"blk": other}, device_id_type=MESH)

    own = [
        pltpu.make_async_copy(src, dst, local_sem.at[i])
        for i, (src, dst) in enumerate((
            (len_hbm, len_ref),
            (qreq_hbm, qreq_ref),
            (qoff_hbm, qoff_ref),
            (sreq_hbm, sreq_ref),
            (spos_hbm, spos_ref),
            (q_hbm, qs.at[0, :, pl.ds(0, QW)]),
            (k_hbm, ks.at[0]),
            (v_hbm, vs.at[0, :, pl.ds(0, HD)]),
        ))
    ]
    for copy in own:
        copy.start()
    for copy in own[:5]:
        copy.wait()

    request = qreq_ref[...]
    length = jnp.where(request == 0, len_ref[0], len_ref[1])
    position = length - 1 - qoff_ref[...]
    eye = lax.broadcasted_iota(jnp.int32, (TOK, TOK), 0) == lax.broadcasted_iota(jnp.int32, (TOK, TOK), 1)

    def column(row):
        return jnp.sum(jnp.where(eye, jnp.broadcast_to(row, (TOK, TOK)), 0), axis=1, keepdims=True)

    lane = lax.broadcasted_iota(jnp.int32, (TOK, HD), 1)
    position = column(position)
    meta = jnp.where(
        lane == 0, column(request),
        jnp.where(lane == 1, position // 128, jnp.where(lane == 2, position % 128, 0)),
    )
    qs[0, :, QW:] = meta.astype(F32).astype(BF16)
    code[0] = sreq_ref[...].astype(F32) * REQ_STEP + spos_ref[...].astype(F32)
    for copy in own[5:]:
        copy.wait()
    pl.semaphore_wait(barrier, 7)

    def remote(src, dst, send_sem, recv_sem, other):
        return pltpu.make_async_remote_copy(
            src_ref=src, dst_ref=dst, send_sem=send_sem, recv_sem=recv_sem,
            device_id={"blk": other}, device_id_type=MESH,
        )

    def kv_copies(chunk, src_slot, src_at, dst_slot, dst_at, other):
        src = pl.ds(src_at, HALF)
        dst = pl.ds(dst_at, HALF)
        return [
            remote(ks.at[src_slot, src], ks.at[dst_slot, dst],
                   kv_send.at[chunk, 0], kv_recv.at[chunk, 0], other),
            remote(vs.at[src_slot, src, pl.ds(0, HD)], vs.at[dst_slot, dst, pl.ds(0, HD)],
                   kv_send.at[chunk, 1], kv_recv.at[chunk, 1], other),
            remote(code.at[src_slot, :, src], code.at[dst_slot, :, dst],
                   kv_send.at[chunk, 2], kv_recv.at[chunk, 2], other),
        ]

    kv = [
        kv_copies(0, 0, HALF, 1, 0, right),
        kv_copies(1, 0, 0, 1, HALF, left),
        kv_copies(2, 0, 0, 2, 0, right),
        kv_copies(3, 0, HALF, 2, HALF, left),
        kv_copies(4, 1, 0, 3, HALF, right),
        kv_copies(5, 1, HALF, 3, 0, left),
    ]

    def q_copy(src_slot, dst_slot, begin, count, sem, other):
        rows = pl.ds(begin, count)
        return remote(qs.at[src_slot, rows], qs.at[dst_slot, rows], q_send.at[sem], q_recv.at[sem], other)

    q_low = q_copy(0, 7, 0, TOK, 7, up)
    q_high = q_copy(0, 1, 0, TOK, 1, down)
    q_far = q_copy(0, 4, 0, TOK, 4, far)
    q_low2 = q_copy(7, 6, 0, TOK, 6, up)
    q_high2 = q_copy(1, 2, 0, TOK, 2, down)
    q_low3 = q_copy(7, 5, 0, TOK, 5, up2)
    q_high3 = q_copy(1, 3, 0, TOK, 3, down2)
    qc = [q_low, q_high, q_far, q_low2, q_high2, q_low3, q_high3]

    def part_copies(src_slot, dst_slot, other):
        return [
            remote(sent.at[src_slot], got.at[dst_slot],
                   part_send.at[dst_slot, 0], part_recv.at[dst_slot, 0], other),
            remote(sent_stat.at[src_slot], got_stat.at[dst_slot],
                   part_send.at[dst_slot, 1], part_recv.at[dst_slot, 1], other),
        ]

    part = {
        1: part_copies(1, 0, up),
        7: part_copies(7, 1, down),
        2: part_copies(2, 2, up2),
        6: part_copies(6, 3, down2),
        4: part_copies(4, 4, far),
        3: part_copies(3, 5, up),
        5: part_copies(5, 6, down),
    }

    def start(copies):
        for copy in copies:
            copy.start()

    start([q_low, q_high])
    start(kv[0])
    start(kv[1])
    start([q_far])
    start(kv[2])
    start(kv[3])

    vs[:, :, HD:] = jnp.ones((NX, SLOT, HD), BF16)
    eye_hd = lax.broadcasted_iota(jnp.int32, (HD, HD), 0) == lax.broadcasted_iota(jnp.int32, (HD, HD), 1)

    def to_row(block):
        return jnp.sum(jnp.where(eye_hd, block, 0.0), axis=0, keepdims=True)

    def to_column(row):
        return jnp.sum(jnp.where(eye_hd, jnp.broadcast_to(row, (HD, HD)), 0.0), axis=1, keepdims=True)

    def state(query, g):
        rows = pl.ds(g * HD, HD)
        return peak[query, rows, :], acc[query, rows, 0:HD], acc[query, rows, HD:]

    def merge(mine, slot, g):
        rows = pl.ds(g * HD, HD)
        m, w, l = mine
        m_in = to_column(got_stat[slot, g, 0:1, :])
        l_in = to_column(got_stat[slot, g, 1:2, :])
        m_new = jnp.maximum(m, m_in)
        keep = jnp.exp2(m - m_new)
        take = jnp.exp2(m_in - m_new)
        return m_new, w * keep + got[slot, rows, :].astype(F32) * take, l * keep + l_in * take

    def finish(query):
        arrived = {2: (3, 5), 6: (5, 6)}.get(query)
        if arrived:
            for copy in part[arrived[0]]:
                copy.wait_recv()
        for g in range(4):
            now = state(query, g)
            if arrived:
                now = merge(now, arrived[1], g)
            m, w, l = now
            sent[query, pl.ds(g * HD, HD), :] = w.astype(BF16)
            sent_stat[query, g, 0:1, :] = to_row(m)
            sent_stat[query, g, 1:2, :] = to_row(l)
        start(part[query])

    actions = {}

    def at(stage, action):
        actions.setdefault(stage, []).append(action)

    def take_query(arriving, forward):
        def action():
            for copy in arriving:
                copy.wait_recv()
            start(forward)
        return action

    def take_keys(*chunks):
        def action():
            for chunk in chunks:
                kv[chunk][0].wait_recv()
                kv[chunk][2].wait_recv()
        return action

    def take_values(*chunks):
        def action():
            for chunk in chunks:
                kv[chunk][1].wait_recv()
        return action

    def send_on():
        start(kv[4])
        start(kv[5])

    at(first_use(0, 1) - 1, take_query([q_low, q_high], [q_low3, q_high3, q_low2, q_high2]))
    at(first_use(0, 2) - 1, take_query([q_low2, q_high2], []))
    at(first_use(0, 3) - 1, take_query([q_low3, q_high3], []))
    at(first_use(0, 4) - 1, take_query([q_far], []))
    for key, chunks in ((1, (0, 1)), (2, (2, 3)), (3, (4, 5))):
        at(first_use(1, key) - 1, take_keys(*chunks))
        at(first_use(1, key) + 1, take_values(*chunks))
    at(first_use(1, 1) + 1, send_on)
    for query in (3, 5, 4, 1, 7, 2, 6):
        at(last_use(query) + 2, functools.partial(finish, query))

    def scores(query, key, into):
        q = jnp.concatenate([qs[query, :, pl.ds(h * HD, HD)] for h in range(QH_DEV)], axis=0)
        into[...] = lax.dot_general(q, ks[key], (((1,), (1,)), ((), ())), preferred_element_type=F32)

    def mask(query, key, into):
        meta = qs[query, :, QW:].astype(F32)
        low = meta[:, 0:1] * REQ_STEP
        high = low + (meta[:, 1:2] * 128.0 + meta[:, 2:3])
        where = code[key]
        into[...] = jnp.where((where >= low) & (where <= high), 0.0, MASKED)

    def softmax(query, key, scored, masked, weights, shrink):
        bias = masked[...]
        for r in range(ROWS // SOFT_ROWS):
            rows = pl.ds(r * SOFT_ROWS, SOFT_ROWS)
            heads = SOFT_ROWS // TOK
            s = (scored[rows, :].reshape(heads, TOK, SLOT) * SCALE + bias[None]).reshape(SOFT_ROWS, SLOT)
            top = jnp.max(s, axis=1, keepdims=True)
            if key == 0:
                m_new = jnp.broadcast_to(jnp.maximum(top, FLOOR), (SOFT_ROWS, HD))
            else:
                m_old = peak[query, rows, :]
                m_new = jnp.maximum(m_old, top)
                shrink[rows, :] = jnp.exp2(m_old - m_new)
            weights[rows, :] = jnp.exp2(s - m_new[:, 0:1]).astype(BF16)
            peak[query, rows, :] = m_new

    def values(query, key, weights, shrink):
        o = jnp.dot(weights[...], vs[key], preferred_element_type=F32)
        if key == 0:
            acc[query] = o
        else:
            keep = shrink[...]
            acc[query, :, 0:HD] = acc[query, :, 0:HD] * keep + o[:, 0:HD]
            acc[query, :, HD:] = acc[query, :, HD:] * keep + o[:, HD:]

    scores(*PAIRS[0], s0)
    mask(*PAIRS[0], b0)
    buffers = ((s0, b0, p0, a0), (s1, b1, p1, a1))
    for i in range(N):
        for action in actions.get(i, ()):
            action()
        (s_now, b_now, p_now, a_now), (s_next, b_next, p_last, a_last) = buffers[i % 2], buffers[1 - i % 2]
        if i + 1 < N:
            scores(*PAIRS[i + 1], s_next)
            mask(*PAIRS[i + 1], b_next)
        softmax(*PAIRS[i], s_now, b_now, p_now, a_now)
        if i:
            values(*PAIRS[i - 1], p_last, a_last)
    values(*PAIRS[N - 1], p1, a1)

    for query in (4, 2, 6, 1, 7):
        for copy in part[query]:
            copy.wait_recv()
    for g in range(4):
        now = state(0, g)
        for slot in range(5):
            now = merge(now, slot, g)
        o = (now[1] / now[2]).astype(BF16)
        for h in range(4):
            out_ref[:, pl.ds((g * 4 + h) * HD, HD)] = o[h * TOK:(h + 1) * TOK, :]

    for copies in kv:
        for copy in copies:
            copy.wait_send()
    for copy in qc:
        copy.wait_send()
    for copies in part.values():
        for copy in copies:
            copy.wait_send()


def shards(
    queries,
    cache_keys,
    cache_values,
    slot_request,
    slot_position,
    lengths,
    query_request,
    query_offset,
):
    vmem = pl.BlockSpec(memory_space=pltpu.VMEM)
    hbm = pl.BlockSpec(memory_space=pltpu.HBM)
    dma = pltpu.SemaphoreType.DMA
    return pl.pallas_call(
        kernel,
        out_shape=jax.ShapeDtypeStruct((TOK, QW), BF16),
        in_specs=[hbm] * 8,
        out_specs=vmem,
        scratch_shapes=[
            pltpu.SMEM((2,), jnp.int32),
            pltpu.VMEM((1, TOK), jnp.int32),
            pltpu.VMEM((1, TOK), jnp.int32),
            pltpu.VMEM((1, SLOT), jnp.int32),
            pltpu.VMEM((1, SLOT), jnp.int32),
            pltpu.VMEM((NZ, TOK, QW + HD), BF16),
            pltpu.VMEM((NX, SLOT, HD), BF16),
            pltpu.VMEM((NX, SLOT, 2 * HD), BF16),
            pltpu.VMEM((NX, 1, SLOT), F32),
            pltpu.VMEM((TOK, SLOT), F32),
            pltpu.VMEM((TOK, SLOT), F32),
            pltpu.VMEM((ROWS, SLOT), F32),
            pltpu.VMEM((ROWS, SLOT), F32),
            pltpu.VMEM((ROWS, SLOT), BF16),
            pltpu.VMEM((ROWS, SLOT), BF16),
            pltpu.VMEM((ROWS, HD), F32),
            pltpu.VMEM((ROWS, HD), F32),
            pltpu.VMEM((NZ, ROWS, 2 * HD), F32),
            pltpu.VMEM((NZ, ROWS, HD), F32),
            pltpu.VMEM((NZ, ROWS, HD), BF16),
            pltpu.VMEM((NZ, 4, 8, HD), F32),
            pltpu.VMEM((NZ, ROWS, HD), BF16),
            pltpu.VMEM((NZ, 4, 8, HD), F32),
            dma((8,)),
            dma((6, 3)),
            dma((6, 3)),
            dma((NZ,)),
            dma((NZ,)),
            dma((NZ, 2)),
            dma((NZ, 2)),
        ],
        compiler_params=pltpu.CompilerParams(
            collective_id=0, has_side_effects=True, vmem_limit_bytes=63 * 2 ** 20
        ),
        cost_estimate=pl.CostEstimate(
            flops=4 * ROWS * SLOT * HD * N, bytes_accessed=2 ** 20, transcendentals=ROWS * SLOT * N
        ),
        name="ring_attention",
    )(
        lengths,
        query_request.reshape(1, TOK),
        query_offset.reshape(1, TOK),
        slot_request.reshape(1, SLOT),
        slot_position.reshape(1, SLOT),
        queries,
        cache_keys,
        cache_values,
    )


def solution(mesh):
    return jax.shard_map(
        shards,
        mesh=mesh,
        in_specs=(
            P(("rep", "blk"), "head"),
            P(("rep", "blk"), "head"),
            P(("rep", "blk"), "head"),
            P(("rep", "blk")),
            P(("rep", "blk")),
            P("rep"),
            P(("rep", "blk")),
            P(("rep", "blk")),
        ),
        out_specs=P(("rep", "blk"), "head"),
        check_vma=False,
    )
```

```python
import functools

import jax
import jax.numpy as jnp
from jax import lax
from jax.experimental import pallas as pl
from jax.experimental.pallas import tpu as pltpu
from jax.sharding import PartitionSpec as P

HD = 128
QH_DEV = 16
TOK = 32
ROWS = TOK * QH_DEV
SLOT = 1024
HALF = SLOT // 2
QW = QH_DEV * HD
NZ = 8
NX = 4
SCALE = 1.4426950408889634 * HD ** -0.5
MASKED = -1e30
FLOOR = -1e29
REQ_STEP = 65536.0
SOFT_ROWS = 128
MESH = pl.DeviceIdType.MESH
F32 = jnp.float32
BF16 = jnp.bfloat16

PAIRS = (
    (0, 0), (1, 0), (7, 0), (1, 1), (7, 1), (0, 1), (3, 0), (5, 0),
    (3, 1), (5, 1), (3, 2), (5, 2), (4, 0), (4, 1), (4, 2), (3, 3),
    (5, 3), (4, 3), (2, 0), (6, 0), (2, 1), (6, 1), (2, 2), (6, 2),
    (2, 3), (6, 3), (1, 2), (1, 3), (7, 2), (7, 3), (0, 2), (0, 3),
)
N = len(PAIRS)


def first_use(kind, value):
    return min(i for i, pair in enumerate(PAIRS) if pair[kind] == value)


def last_use(query):
    return max(i for i, pair in enumerate(PAIRS) if pair[0] == query)


def kernel(
    len_hbm, qreq_hbm, qoff_hbm, sreq_hbm, spos_hbm, q_hbm, k_hbm, v_hbm,
    out_ref,
    len_ref, qreq_ref, qoff_ref, sreq_ref, spos_ref,
    qs, ks, vs, code, b0, b1, s0, s1, p0, p1, a0, a1, acc, peak,
    sent, sent_stat, got, got_stat,
    local_sem, kv_send, kv_recv, q_send, q_recv, part_send, part_recv,
):
    me = lax.axis_index("blk")
    z = me // NX
    x = lax.rem(me, NX)

    def along_z(step):
        return lax.rem(z + step + NZ, NZ) * NX + x

    right = z * NX + lax.rem(x + 1, NX)
    left = z * NX + lax.rem(x + NX - 1, NX)
    up, up2, down2, down = (along_z(step) for step in (1, 2, -2, -1))

    barrier = pltpu.get_barrier_semaphore()
    for other in (up, down, right, left, up2, down2):
        pl.semaphore_signal(barrier, inc=1, device_id={"blk": other}, device_id_type=MESH)

    own = [
        pltpu.make_async_copy(src, dst, local_sem.at[i])
        for i, (src, dst) in enumerate((
            (len_hbm, len_ref),
            (qreq_hbm, qreq_ref),
            (qoff_hbm, qoff_ref),
            (sreq_hbm, sreq_ref),
            (spos_hbm, spos_ref),
            (q_hbm, qs.at[0, :, pl.ds(0, QW)]),
            (k_hbm, ks.at[0]),
            (v_hbm, vs.at[0]),
        ))
    ]
    for copy in own:
        copy.start()
    for copy in own[:5]:
        copy.wait()

    request = qreq_ref[...]
    length = jnp.where(request == 0, len_ref[0], len_ref[1])
    position = length - 1 - qoff_ref[...]
    eye = lax.broadcasted_iota(jnp.int32, (TOK, TOK), 0) == lax.broadcasted_iota(jnp.int32, (TOK, TOK), 1)

    def column(row):
        return jnp.sum(jnp.where(eye, jnp.broadcast_to(row, (TOK, TOK)), 0), axis=1, keepdims=True)

    lane = lax.broadcasted_iota(jnp.int32, (TOK, HD), 1)
    position = column(position)
    meta = jnp.where(
        lane == 0, column(request),
        jnp.where(lane == 1, position // 128, jnp.where(lane == 2, position % 128, 0)),
    )
    qs[0, :, QW:] = meta.astype(F32).astype(BF16)
    code[0] = sreq_ref[...].astype(F32) * REQ_STEP + spos_ref[...].astype(F32)
    def scores(query, key, into):
        q = jnp.concatenate([qs[query, :, pl.ds(h * HD, HD)] for h in range(QH_DEV)], axis=0)
        into[...] = lax.dot_general(q, ks[key], (((1,), (1,)), ((), ())), preferred_element_type=F32)

    def mask(query, key, into):
        meta = qs[query, :, QW:].astype(F32)
        low = meta[:, 0:1] * REQ_STEP
        high = low + (meta[:, 1:2] * 128.0 + meta[:, 2:3])
        where = code[key]
        into[...] = jnp.where((where >= low) & (where <= high), 0.0, MASKED)

    def softmax(query, key, scored, masked, weights, shrink):
        bias = masked[...]
        for r in range(ROWS // SOFT_ROWS):
            rows = pl.ds(r * SOFT_ROWS, SOFT_ROWS)
            heads = SOFT_ROWS // TOK
            s = (scored[rows, :].reshape(heads, TOK, SLOT) * SCALE + bias[None]).reshape(SOFT_ROWS, SLOT)
            top = jnp.max(s, axis=1, keepdims=True)
            if key == 0:
                m_new = jnp.broadcast_to(jnp.maximum(top, FLOOR), (SOFT_ROWS, HD))
            else:
                m_old = peak[query, rows, :]
                m_new = jnp.maximum(m_old, top)
                shrink[rows, :] = jnp.exp2(m_old - m_new)
            weights[rows, :] = jnp.exp2(s - m_new[:, 0:1]).astype(BF16)
            peak[query, rows, :] = m_new

    def values(query, key, weights, shrink):
        columns = jnp.concatenate([vs[key], jnp.ones((SLOT, HD), BF16)], axis=1)
        o = jnp.dot(weights[...], columns, preferred_element_type=F32)
        if key == 0:
            acc[query] = o
        else:
            keep = shrink[...]
            acc[query, :, 0:HD] = acc[query, :, 0:HD] * keep + o[:, 0:HD]
            acc[query, :, HD:] = acc[query, :, HD:] * keep + o[:, HD:]

    for copy in own[5:]:
        copy.wait()
    scores(*PAIRS[0], s0)
    mask(*PAIRS[0], b0)
    softmax(*PAIRS[0], s0, b0, p0, a0)
    pl.semaphore_wait(barrier, 6)

    def remote(src, dst, send_sem, recv_sem, other):
        return pltpu.make_async_remote_copy(
            src_ref=src, dst_ref=dst, send_sem=send_sem, recv_sem=recv_sem,
            device_id={"blk": other}, device_id_type=MESH,
        )

    def kv_copies(chunk, src_slot, src_at, dst_slot, dst_at, other):
        src = pl.ds(src_at, HALF)
        dst = pl.ds(dst_at, HALF)
        return [
            remote(ks.at[src_slot, src], ks.at[dst_slot, dst],
                   kv_send.at[chunk, 0], kv_recv.at[chunk, 0], other),
            remote(vs.at[src_slot, src], vs.at[dst_slot, dst],
                   kv_send.at[chunk, 1], kv_recv.at[chunk, 1], other),
            remote(code.at[src_slot, :, src], code.at[dst_slot, :, dst],
                   kv_send.at[chunk, 2], kv_recv.at[chunk, 2], other),
        ]

    kv = [
        kv_copies(0, 0, HALF, 1, 0, right),
        kv_copies(1, 0, 0, 1, HALF, left),
        kv_copies(2, 0, 0, 2, 0, right),
        kv_copies(3, 0, HALF, 2, HALF, left),
        kv_copies(4, 1, 0, 3, HALF, right),
        kv_copies(5, 1, HALF, 3, 0, left),
    ]

    def q_copy(src_slot, dst_slot, begin, count, sem, other):
        rows = pl.ds(begin, count)
        return remote(qs.at[src_slot, rows], qs.at[dst_slot, rows], q_send.at[sem], q_recv.at[sem], other)

    q_low = q_copy(0, 7, 0, TOK, 7, up)
    q_high = q_copy(0, 1, 0, TOK, 1, down)
    q_low3 = q_copy(7, 5, 0, TOK, 5, up2)
    q_high3 = q_copy(1, 3, 0, TOK, 3, down2)
    q_low2 = q_copy(7, 6, 0, TOK, 6, up)
    q_high2 = q_copy(1, 2, 0, TOK, 2, down)
    q_low4 = q_copy(5, 4, 0, TOK // 2, 4, up)
    q_high4 = q_copy(3, 4, TOK // 2, TOK // 2, 0, down)
    qc = [q_low, q_high, q_low3, q_high3, q_low2, q_high2, q_low4, q_high4]

    def part_copies(src_slot, dst_slot, other, begin=0, count=ROWS):
        rows = pl.ds(begin, count)
        stats = pl.ds(begin // HD, count // HD)
        return [
            remote(sent.at[src_slot, rows], got.at[dst_slot, rows],
                   part_send.at[dst_slot, 0], part_recv.at[dst_slot, 0], other),
            remote(sent_stat.at[src_slot, stats], got_stat.at[dst_slot, stats],
                   part_send.at[dst_slot, 1], part_recv.at[dst_slot, 1], other),
        ]

    part = {
        1: {0: part_copies(1, 0, up)},
        7: {1: part_copies(7, 1, down)},
        2: {2: part_copies(2, 2, up2)},
        6: {3: part_copies(6, 3, down2)},
        3: {5: part_copies(3, 5, up)},
        5: {6: part_copies(5, 6, down)},
        4: {4: part_copies(4, 4, up2, 0, ROWS // 2),
            7: part_copies(4, 7, down2, ROWS // 2, ROWS // 2)},
    }
    parts = {slot: copies for slots in part.values() for slot, copies in slots.items()}

    def start(copies):
        for copy in copies:
            copy.start()

    start([q_low, q_high])
    start(kv[0])
    start(kv[1])

    eye_hd = lax.broadcasted_iota(jnp.int32, (HD, HD), 0) == lax.broadcasted_iota(jnp.int32, (HD, HD), 1)

    def to_row(block):
        return jnp.sum(jnp.where(eye_hd, block, 0.0), axis=0, keepdims=True)

    def to_column(row):
        return jnp.sum(jnp.where(eye_hd, jnp.broadcast_to(row, (HD, HD)), 0.0), axis=1, keepdims=True)

    def state(query, g):
        rows = pl.ds(g * HD, HD)
        return peak[query, rows, :], acc[query, rows, 0:HD], acc[query, rows, HD:]

    def merge(mine, slot, g):
        rows = pl.ds(g * HD, HD)
        m, w, l = mine
        m_in = to_column(got_stat[slot, g, 0:1, :])
        l_in = to_column(got_stat[slot, g, 1:2, :])
        m_new = jnp.maximum(m, m_in)
        keep = jnp.exp2(m - m_new)
        take = jnp.exp2(m_in - m_new)
        return m_new, w * keep + got[slot, rows, :].astype(F32) * take, l * keep + l_in * take

    def finish(query):
        arrived = {2: {5: (0, 1, 2, 3), 4: (0, 1)}, 6: {6: (0, 1, 2, 3), 7: (2, 3)}}.get(query, {})
        for slot in arrived:
            for copy in parts[slot]:
                copy.wait_recv()
        for g in range(4):
            now = state(query, g)
            for slot, groups in arrived.items():
                if g in groups:
                    now = merge(now, slot, g)
            m, w, l = now
            sent[query, pl.ds(g * HD, HD), :] = w.astype(BF16)
            sent_stat[query, g, 0:1, :] = to_row(m)
            sent_stat[query, g, 1:2, :] = to_row(l)
        for copies in part[query].values():
            start(copies)

    actions = {}

    def at(stage, action):
        actions.setdefault(stage, []).append(action)

    def take_queries(*arriving):
        for copy in arriving:
            copy.wait_recv()

    def take_keys(*chunks):
        for chunk in chunks:
            for copy in kv[chunk]:
                copy.wait_recv()

    at(first_use(0, 1) - 1, lambda: take_queries(q_low, q_high))
    at(first_use(0, 1) - 1, lambda: start([q_low3, q_high3] + kv[2] + kv[3]))
    at(first_use(1, 1) - 1, lambda: take_keys(0, 1))
    at(first_use(1, 1) - 1, lambda: start(kv[4] + kv[5]))
    at(first_use(0, 3) - 1, lambda: take_queries(q_low3, q_high3))
    at(first_use(0, 3) - 1, lambda: start([q_low2, q_high2, q_low4, q_high4]))
    at(first_use(1, 2) - 1, lambda: take_keys(2, 3))
    at(first_use(0, 4) - 1, lambda: take_queries(q_low4, q_high4))
    at(first_use(1, 3) - 1, lambda: take_keys(4, 5))
    at(first_use(0, 2) - 1, lambda: take_queries(q_low2, q_high2))
    for query in (3, 5, 4, 2, 6, 1, 7):
        at(last_use(query) + 2 + (query == 3), functools.partial(finish, query))

    buffers = ((s0, b0, p0, a0), (s1, b1, p1, a1))
    for i in range(N):
        for action in actions.get(i, ()):
            action()
        (s_now, b_now, p_now, a_now), (s_next, b_next, p_last, a_last) = buffers[i % 2], buffers[1 - i % 2]
        if i + 1 < N:
            scores(*PAIRS[i + 1], s_next)
            mask(*PAIRS[i + 1], b_next)
        if i:
            softmax(*PAIRS[i], s_now, b_now, p_now, a_now)
            values(*PAIRS[i - 1], p_last, a_last)
    values(*PAIRS[N - 1], p1, a1)

    for slot in range(4):
        for copy in parts[slot]:
            copy.wait_recv()
    for g in range(4):
        now = state(0, g)
        for slot in range(4):
            now = merge(now, slot, g)
        o = (now[1] / now[2]).astype(BF16)
        for h in range(4):
            out_ref[:, pl.ds((g * 4 + h) * HD, HD)] = o[h * TOK:(h + 1) * TOK, :]

    for copies in kv:
        for copy in copies:
            copy.wait_send()
    for copy in qc:
        copy.wait_send()
    for copies in parts.values():
        for copy in copies:
            copy.wait_send()


def shards(
    queries,
    cache_keys,
    cache_values,
    slot_request,
    slot_position,
    lengths,
    query_request,
    query_offset,
):
    vmem = pl.BlockSpec(memory_space=pltpu.VMEM)
    hbm = pl.BlockSpec(memory_space=pltpu.HBM)
    dma = pltpu.SemaphoreType.DMA
    return pl.pallas_call(
        kernel,
        out_shape=jax.ShapeDtypeStruct((TOK, QW), BF16),
        in_specs=[hbm] * 8,
        out_specs=vmem,
        scratch_shapes=[
            pltpu.SMEM((2,), jnp.int32),
            pltpu.VMEM((1, TOK), jnp.int32),
            pltpu.VMEM((1, TOK), jnp.int32),
            pltpu.VMEM((1, SLOT), jnp.int32),
            pltpu.VMEM((1, SLOT), jnp.int32),
            pltpu.VMEM((NZ, TOK, QW + HD), BF16),
            pltpu.VMEM((NX, SLOT, HD), BF16),
            pltpu.VMEM((NX, SLOT, HD), BF16),
            pltpu.VMEM((NX, 1, SLOT), F32),
            pltpu.VMEM((TOK, SLOT), F32),
            pltpu.VMEM((TOK, SLOT), F32),
            pltpu.VMEM((ROWS, SLOT), F32),
            pltpu.VMEM((ROWS, SLOT), F32),
            pltpu.VMEM((ROWS, SLOT), BF16),
            pltpu.VMEM((ROWS, SLOT), BF16),
            pltpu.VMEM((ROWS, HD), F32),
            pltpu.VMEM((ROWS, HD), F32),
            pltpu.VMEM((NZ, ROWS, 2 * HD), F32),
            pltpu.VMEM((NZ, ROWS, HD), F32),
            pltpu.VMEM((NZ, ROWS, HD), BF16),
            pltpu.VMEM((NZ, 4, 8, HD), F32),
            pltpu.VMEM((NZ, ROWS, HD), BF16),
            pltpu.VMEM((NZ, 4, 8, HD), F32),
            dma((8,)),
            dma((6, 3)),
            dma((6, 3)),
            dma((NZ,)),
            dma((NZ,)),
            dma((NZ, 2)),
            dma((NZ, 2)),
        ],
        compiler_params=pltpu.CompilerParams(
            collective_id=0, has_side_effects=True, vmem_limit_bytes=63 * 2 ** 20
        ),
        cost_estimate=pl.CostEstimate(
            flops=4 * ROWS * SLOT * HD * N, bytes_accessed=2 ** 20, transcendentals=ROWS * SLOT * N
        ),
        name="ring_attention",
    )(
        lengths,
        query_request.reshape(1, TOK),
        query_offset.reshape(1, TOK),
        slot_request.reshape(1, SLOT),
        slot_position.reshape(1, SLOT),
        queries,
        cache_keys,
        cache_values,
    )


def solution(mesh):
    return jax.shard_map(
        shards,
        mesh=mesh,
        in_specs=(
            P(("rep", "blk"), "head"),
            P(("rep", "blk"), "head"),
            P(("rep", "blk"), "head"),
            P(("rep", "blk")),
            P(("rep", "blk")),
            P("rep"),
            P(("rep", "blk")),
            P(("rep", "blk")),
        ),
        out_specs=P(("rep", "blk"), "head"),
        check_vma=False,
    )
```

```python
import functools

import jax
import jax.numpy as jnp
from jax import lax
from jax.experimental import pallas as pl
from jax.experimental.pallas import tpu as pltpu
from jax.sharding import PartitionSpec as P

HD = 128
QH_DEV = 16
TOK = 32
ROWS = TOK * QH_DEV
SLOT = 1024
HALF = SLOT // 2
QW = QH_DEV * HD
NZ = 8
NX = 4
SCALE = 1.4426950408889634 * HD ** -0.5
MASKED = -1e30
FLOOR = -1e29
REQ_STEP = 65536.0
SOFT_ROWS = 128
MESH = pl.DeviceIdType.MESH
F32 = jnp.float32
BF16 = jnp.bfloat16

PAIRS = (
    (0, 0), (1, 0), (7, 0), (1, 1), (7, 1), (0, 1), (3, 0), (5, 0),
    (3, 1), (5, 1), (3, 2), (5, 2), (4, 0), (4, 1), (4, 2), (3, 3),
    (5, 3), (4, 3), (2, 0), (6, 0), (2, 1), (6, 1), (2, 2), (6, 2),
    (2, 3), (6, 3), (1, 2), (1, 3), (7, 2), (7, 3), (0, 2), (0, 3),
)
N = len(PAIRS)
FINISH = ((3, 18), (5, 18), (4, 19), (2, 26), (6, 27), (1, 29), (7, 31))
ARRIVALS = (2, 3, 0, 1)


def first_use(kind, value):
    return min(i for i, pair in enumerate(PAIRS) if pair[kind] == value)


def last_use(query):
    return max(i for i, pair in enumerate(PAIRS) if pair[0] == query)


def kernel(
    len_hbm, qreq_hbm, qoff_hbm, sreq_hbm, spos_hbm, q_hbm, k_hbm, v_hbm,
    out_ref,
    len_ref, qreq_ref, qoff_ref, sreq_ref, spos_ref,
    qs, ks, vs, code, b0, b1, s0, s1, p0, p1, a0, a1, acc, peak,
    sent, sent_stat, got, got_stat,
    local_sem, kv_send, kv_recv, q_send, q_recv, part_send, part_recv,
):
    me = lax.axis_index("blk")
    z = me // NX
    x = lax.rem(me, NX)

    def along_z(step):
        return lax.rem(z + step + NZ, NZ) * NX + x

    right = z * NX + lax.rem(x + 1, NX)
    left = z * NX + lax.rem(x + NX - 1, NX)
    up, up2, down2, down = (along_z(step) for step in (1, 2, -2, -1))

    barrier = pltpu.get_barrier_semaphore()
    for other in (up, down, right, left, up2, down2):
        pl.semaphore_signal(barrier, inc=1, device_id={"blk": other}, device_id_type=MESH)

    own = [
        pltpu.make_async_copy(src, dst, local_sem.at[i])
        for i, (src, dst) in enumerate((
            (len_hbm, len_ref),
            (qreq_hbm, qreq_ref),
            (qoff_hbm, qoff_ref),
            (sreq_hbm, sreq_ref),
            (spos_hbm, spos_ref),
            (q_hbm, qs.at[0, :, pl.ds(0, QW)]),
            (k_hbm, ks.at[0]),
            (v_hbm, vs.at[0]),
        ))
    ]
    for copy in own:
        copy.start()
    for copy in own[:5]:
        copy.wait()

    request = qreq_ref[...]
    length = jnp.where(request == 0, len_ref[0], len_ref[1])
    position = length - 1 - qoff_ref[...]
    eye = lax.broadcasted_iota(jnp.int32, (TOK, TOK), 0) == lax.broadcasted_iota(jnp.int32, (TOK, TOK), 1)

    def column(row):
        return jnp.sum(jnp.where(eye, jnp.broadcast_to(row, (TOK, TOK)), 0), axis=1, keepdims=True)

    lane = lax.broadcasted_iota(jnp.int32, (TOK, HD), 1)
    position = column(position)
    meta = jnp.where(
        lane == 0, column(request),
        jnp.where(lane == 1, position // 128, jnp.where(lane == 2, position % 128, 0)),
    )
    qs[0, :, QW:] = meta.astype(F32).astype(BF16)
    code[0] = sreq_ref[...].astype(F32) * REQ_STEP + spos_ref[...].astype(F32)
    def scores(query, key, into):
        q = jnp.concatenate([qs[query, :, pl.ds(h * HD, HD)] for h in range(QH_DEV)], axis=0)
        into[...] = lax.dot_general(q, ks[key], (((1,), (1,)), ((), ())), preferred_element_type=F32)

    def mask(query, key, into):
        meta = qs[query, :, QW:].astype(F32)
        low = meta[:, 0:1] * REQ_STEP
        high = low + (meta[:, 1:2] * 128.0 + meta[:, 2:3])
        where = code[key]
        into[...] = jnp.where((where >= low) & (where <= high), 0.0, MASKED)

    def softmax(query, key, scored, masked, weights, shrink):
        bias = masked[...]
        for r in range(ROWS // SOFT_ROWS):
            rows = pl.ds(r * SOFT_ROWS, SOFT_ROWS)
            heads = SOFT_ROWS // TOK
            s = (scored[rows, :].reshape(heads, TOK, SLOT) * SCALE + bias[None]).reshape(SOFT_ROWS, SLOT)
            top = jnp.max(s, axis=1, keepdims=True)
            if key == 0:
                m_new = jnp.broadcast_to(jnp.maximum(top, FLOOR), (SOFT_ROWS, HD))
            else:
                m_old = peak[query, rows, :]
                m_new = jnp.maximum(m_old, top)
                shrink[rows, :] = jnp.exp2(m_old - m_new)
            weights[rows, :] = jnp.exp2(s - m_new[:, 0:1]).astype(BF16)
            peak[query, rows, :] = m_new

    def values(query, key, weights, shrink):
        columns = jnp.concatenate([vs[key], jnp.ones((SLOT, HD), BF16)], axis=1)
        o = jnp.dot(weights[...], columns, preferred_element_type=F32)
        if key == 0:
            acc[query] = o
        else:
            keep = shrink[...]
            acc[query, :, 0:HD] = acc[query, :, 0:HD] * keep + o[:, 0:HD]
            acc[query, :, HD:] = acc[query, :, HD:] * keep + o[:, HD:]

    for copy in own[5:]:
        copy.wait()
    scores(*PAIRS[0], s0)
    mask(*PAIRS[0], b0)
    softmax(*PAIRS[0], s0, b0, p0, a0)
    pl.semaphore_wait(barrier, 6)

    def remote(src, dst, send_sem, recv_sem, other):
        return pltpu.make_async_remote_copy(
            src_ref=src, dst_ref=dst, send_sem=send_sem, recv_sem=recv_sem,
            device_id={"blk": other}, device_id_type=MESH,
        )

    def kv_copies(chunk, src_slot, src_at, dst_slot, dst_at, other):
        src = pl.ds(src_at, HALF)
        dst = pl.ds(dst_at, HALF)
        return [
            remote(ks.at[src_slot, src], ks.at[dst_slot, dst],
                   kv_send.at[chunk, 0], kv_recv.at[chunk, 0], other),
            remote(vs.at[src_slot, src], vs.at[dst_slot, dst],
                   kv_send.at[chunk, 1], kv_recv.at[chunk, 1], other),
            remote(code.at[src_slot, :, src], code.at[dst_slot, :, dst],
                   kv_send.at[chunk, 2], kv_recv.at[chunk, 2], other),
        ]

    kv = [
        kv_copies(0, 0, HALF, 1, 0, right),
        kv_copies(1, 0, 0, 1, HALF, left),
        kv_copies(2, 0, 0, 2, 0, right),
        kv_copies(3, 0, HALF, 2, HALF, left),
        kv_copies(4, 1, 0, 3, HALF, right),
        kv_copies(5, 1, HALF, 3, 0, left),
    ]

    def q_copy(src_slot, dst_slot, begin, count, sem, other):
        rows = pl.ds(begin, count)
        return remote(qs.at[src_slot, rows], qs.at[dst_slot, rows], q_send.at[sem], q_recv.at[sem], other)

    q_low = q_copy(0, 7, 0, TOK, 7, up)
    q_high = q_copy(0, 1, 0, TOK, 1, down)
    q_low3 = q_copy(7, 5, 0, TOK, 5, up2)
    q_high3 = q_copy(1, 3, 0, TOK, 3, down2)
    q_low2 = q_copy(7, 6, 0, TOK, 6, up)
    q_high2 = q_copy(1, 2, 0, TOK, 2, down)
    q_low4 = q_copy(5, 4, 0, TOK // 2, 4, up)
    q_high4 = q_copy(3, 4, TOK // 2, TOK // 2, 0, down)
    qc = [q_low, q_high, q_low3, q_high3, q_low2, q_high2, q_low4, q_high4]

    def part_copies(src_slot, dst_slot, other, begin=0, count=ROWS):
        rows = pl.ds(begin, count)
        stats = pl.ds(begin // HD, count // HD)
        return [
            remote(sent.at[src_slot, rows], got.at[dst_slot, rows],
                   part_send.at[dst_slot, 0], part_recv.at[dst_slot, 0], other),
            remote(sent_stat.at[src_slot, stats], got_stat.at[dst_slot, stats],
                   part_send.at[dst_slot, 1], part_recv.at[dst_slot, 1], other),
        ]

    part = {
        1: {0: part_copies(1, 0, up)},
        7: {1: part_copies(7, 1, down)},
        2: {2: part_copies(2, 2, up2)},
        6: {3: part_copies(6, 3, down2)},
        3: {5: part_copies(3, 5, up)},
        5: {6: part_copies(5, 6, down)},
        4: {4: part_copies(4, 4, up2, 0, ROWS // 2),
            7: part_copies(4, 7, down2, ROWS // 2, ROWS // 2)},
    }
    parts = {slot: copies for slots in part.values() for slot, copies in slots.items()}

    def start(copies):
        for copy in copies:
            copy.start()

    start([q_low, q_high])
    for part_of in (0, 2, 1):
        start([kv[0][part_of], kv[1][part_of]])

    eye_hd = lax.broadcasted_iota(jnp.int32, (HD, HD), 0) == lax.broadcasted_iota(jnp.int32, (HD, HD), 1)

    def to_row(block):
        return jnp.sum(jnp.where(eye_hd, block, 0.0), axis=0, keepdims=True)

    def to_column(row):
        return jnp.sum(jnp.where(eye_hd, jnp.broadcast_to(row, (HD, HD)), 0.0), axis=1, keepdims=True)

    def state(query, g):
        rows = pl.ds(g * HD, HD)
        return peak[query, rows, :], acc[query, rows, 0:HD], acc[query, rows, HD:]

    def merge(mine, slot, g):
        rows = pl.ds(g * HD, HD)
        m, w, l = mine
        m_in = to_column(got_stat[slot, g, 0:1, :])
        l_in = to_column(got_stat[slot, g, 1:2, :])
        m_new = jnp.maximum(m, m_in)
        keep = jnp.exp2(m - m_new)
        take = jnp.exp2(m_in - m_new)
        return m_new, w * keep + got[slot, rows, :].astype(F32) * take, l * keep + l_in * take

    def finish(query):
        arrived = {2: {5: (0, 1, 2, 3), 4: (0, 1)}, 6: {6: (0, 1, 2, 3), 7: (2, 3)}}.get(query, {})
        for slot in arrived:
            for copy in parts[slot]:
                copy.wait_recv()
        for g in range(4):
            now = state(query, g)
            for slot, groups in arrived.items():
                if g in groups:
                    now = merge(now, slot, g)
            m, w, l = now
            sent[query, pl.ds(g * HD, HD), :] = w.astype(BF16)
            sent_stat[query, g, 0:1, :] = to_row(m)
            sent_stat[query, g, 1:2, :] = to_row(l)
        for copies in part[query].values():
            start(copies)

    actions = {}

    def at(stage, action):
        actions.setdefault(stage, []).append(action)

    def take_queries(*arriving):
        for copy in arriving:
            copy.wait_recv()

    def take_keys(*chunks):
        for chunk in chunks:
            kv[chunk][0].wait_recv()
            kv[chunk][2].wait_recv()

    def take_values(*chunks):
        for chunk in chunks:
            kv[chunk][1].wait_recv()

    at(first_use(0, 1) - 1, lambda: take_queries(q_low, q_high))
    at(first_use(0, 1) - 1, lambda: start(
        [q_low3, q_high3] + [kv[chunk][part_of] for part_of in (0, 2, 1) for chunk in (2, 3)]
    ))
    at(first_use(1, 1) - 1, lambda: take_keys(0, 1))
    at(first_use(1, 1) - 1, lambda: start([kv[4][0], kv[4][2], kv[5][0], kv[5][2]]))
    at(first_use(1, 1) + 1, lambda: take_values(0, 1))
    at(first_use(1, 1) + 1, lambda: start([kv[4][1], kv[5][1]]))
    at(first_use(0, 3) - 1, lambda: take_queries(q_low3, q_high3))
    at(first_use(0, 3) - 1, lambda: start([q_low2, q_high2, q_low4, q_high4]))
    at(first_use(1, 2) - 1, lambda: take_keys(2, 3))
    at(first_use(1, 2) + 1, lambda: take_values(2, 3))
    at(first_use(0, 4) - 1, lambda: take_queries(q_low4, q_high4))
    at(first_use(1, 3) - 1, lambda: take_keys(4, 5))
    at(first_use(1, 3) + 1, lambda: take_values(4, 5))
    at(first_use(0, 2) - 2, lambda: take_queries(q_low2, q_high2))
    for query, stage in FINISH:
        at(stage, functools.partial(finish, query))

    buffers = ((s0, b0, p0, a0), (s1, b1, p1, a1))
    for i in range(N):
        for action in actions.get(i, ()):
            action()
        (s_now, b_now, p_now, a_now), (s_next, b_next, p_last, a_last) = buffers[i % 2], buffers[1 - i % 2]
        if i + 1 < N:
            scores(*PAIRS[i + 1], s_next)
            mask(*PAIRS[i + 1], b_next)
        if i:
            softmax(*PAIRS[i], s_now, b_now, p_now, a_now)
            values(*PAIRS[i - 1], p_last, a_last)
    values(*PAIRS[N - 1], p1, a1)

    for slot in ARRIVALS:
        for copy in parts[slot]:
            copy.wait_recv()
        for g in range(4):
            m, w, l = merge(state(0, g), slot, g)
            rows = pl.ds(g * HD, HD)
            if slot != ARRIVALS[-1]:
                peak[0, rows, :] = m
                acc[0, rows, 0:HD] = w
                acc[0, rows, HD:] = l
                continue
            o = (w / l).astype(BF16)
            for h in range(4):
                out_ref[:, pl.ds((g * 4 + h) * HD, HD)] = o[h * TOK:(h + 1) * TOK, :]

    for copies in kv:
        for copy in copies:
            copy.wait_send()
    for copy in qc:
        copy.wait_send()
    for copies in parts.values():
        for copy in copies:
            copy.wait_send()


def shards(
    queries,
    cache_keys,
    cache_values,
    slot_request,
    slot_position,
    lengths,
    query_request,
    query_offset,
):
    vmem = pl.BlockSpec(memory_space=pltpu.VMEM)
    hbm = pl.BlockSpec(memory_space=pltpu.HBM)
    dma = pltpu.SemaphoreType.DMA
    return pl.pallas_call(
        kernel,
        out_shape=jax.ShapeDtypeStruct((TOK, QW), BF16),
        in_specs=[hbm] * 8,
        out_specs=vmem,
        scratch_shapes=[
            pltpu.SMEM((2,), jnp.int32),
            pltpu.VMEM((1, TOK), jnp.int32),
            pltpu.VMEM((1, TOK), jnp.int32),
            pltpu.VMEM((1, SLOT), jnp.int32),
            pltpu.VMEM((1, SLOT), jnp.int32),
            pltpu.VMEM((NZ, TOK, QW + HD), BF16),
            pltpu.VMEM((NX, SLOT, HD), BF16),
            pltpu.VMEM((NX, SLOT, HD), BF16),
            pltpu.VMEM((NX, 1, SLOT), F32),
            pltpu.VMEM((TOK, SLOT), F32),
            pltpu.VMEM((TOK, SLOT), F32),
            pltpu.VMEM((ROWS, SLOT), F32),
            pltpu.VMEM((ROWS, SLOT), F32),
            pltpu.VMEM((ROWS, SLOT), BF16),
            pltpu.VMEM((ROWS, SLOT), BF16),
            pltpu.VMEM((ROWS, HD), F32),
            pltpu.VMEM((ROWS, HD), F32),
            pltpu.VMEM((NZ, ROWS, 2 * HD), F32),
            pltpu.VMEM((NZ, ROWS, HD), F32),
            pltpu.VMEM((NZ, ROWS, HD), BF16),
            pltpu.VMEM((NZ, 4, 8, HD), F32),
            pltpu.VMEM((NZ, ROWS, HD), BF16),
            pltpu.VMEM((NZ, 4, 8, HD), F32),
            dma((8,)),
            dma((6, 3)),
            dma((6, 3)),
            dma((NZ,)),
            dma((NZ,)),
            dma((NZ, 2)),
            dma((NZ, 2)),
        ],
        compiler_params=pltpu.CompilerParams(
            collective_id=0, has_side_effects=True, vmem_limit_bytes=63 * 2 ** 20
        ),
        cost_estimate=pl.CostEstimate(
            flops=4 * ROWS * SLOT * HD * N, bytes_accessed=2 ** 20, transcendentals=ROWS * SLOT * N
        ),
        name="ring_attention",
    )(
        lengths,
        query_request.reshape(1, TOK),
        query_offset.reshape(1, TOK),
        slot_request.reshape(1, SLOT),
        slot_position.reshape(1, SLOT),
        queries,
        cache_keys,
        cache_values,
    )


def solution(mesh):
    return jax.shard_map(
        shards,
        mesh=mesh,
        in_specs=(
            P(("rep", "blk"), "head"),
            P(("rep", "blk"), "head"),
            P(("rep", "blk"), "head"),
            P(("rep", "blk")),
            P(("rep", "blk")),
            P("rep"),
            P(("rep", "blk")),
            P(("rep", "blk")),
        ),
        out_specs=P(("rep", "blk"), "head"),
        check_vma=False,
    )
```
